512 devices in a mesh: ctx: 128 (over z, y, core), head: 4 (over x).
Axes of the slice: x: 4, y: 8, z: 8, core: 2. Of those that a mesh axis runs over, the one named last changes fastest.
Arguments:
- queries: bfloat16 [49152, 4096], P('ctx', 'head'), may hold values from -6 to 6
- keys: bfloat16 [49152, 1024], P(('ctx', 'head')), may hold values from -6 to 6
- values: bfloat16 [49152, 1024], P(('ctx', 'head')), may hold values from -6 to 6
- doc_lengths: int32 [512], replicated, may hold values from 1 to 1536, 49152 in all
Outputs:
- attended: bfloat16 [49152, 4096], P('ctx', 'head')
The draws below stay inside these ranges and needn't reach their ends.
All inputs are finite; a program needn't handle non-finite values.
Results may differ from the reference program's by a relative error of at most 0.0075.
Values may be sent and summed in bfloat16 or wider, within the bound.
No kernel may reach another device: no remote copies, remote signals or barrier semaphores. Data moves between devices by JAX's collectives and lax.ppermute only.
A program may use at most 128 MiB of HBM per device.

```python
import math
import jax
import jax.numpy as jnp
import numpy as np
from jax import lax

QH = 32
KVH = 8
HD = 128
TOK_DEV = 384
REACH = 4
TOKENS = 49152
MOST = 1536
DOCS = 512


def draw_queries(key, part):
    key = jax.random.fold_in(key, 3)
    base = jnp.clip(jax.random.normal(key, (TOKENS, QH * HD), jnp.float32), -6.0, 6.0)
    return base.astype(jnp.bfloat16)


def draw_keys(key, part):
    key = jax.random.fold_in(key, 5)
    base = jnp.clip(jax.random.normal(key, (TOKENS, KVH * HD), jnp.float32), -6.0, 6.0)
    return base.astype(jnp.bfloat16)


def block_scale(rng, dims, cuts, smallest, top_value):
    level, own = 1.0, jax.random.fold_in(rng, 6)
    for axis_at, parts in cuts:
        draws = jnp.exp(jax.random.uniform(jax.random.fold_in(own, axis_at), (parts,), jnp.float32, smallest / len(cuts), top_value / len(cuts)))
        level = level * jnp.repeat(draws, dims[axis_at] // parts).reshape([-1 if axis == axis_at else 1 for axis in range(len(dims))])
    return level


def split_up(number_of, total, most, lean):
    weights = [(1 << 20) // math.isqrt(standing ** lean) + 1 for standing in range(2, number_of + 1)]
    rest, counts = total - most - (number_of - 1), [1] * (number_of - 1)
    while rest > 0:
        free = [i for i in range(number_of - 1) if counts[i] < most]
        mass, left = sum([weights[i] for i in free]), rest
        for i in free:
            more = min(most - counts[i], max(1, left * weights[i] // mass), rest)
            counts[i] = counts[i] + more
            rest = rest - more
    return np.array([most] + counts)


def uneven(key, count, total, most, skew):
    if count == 2:
        one = jax.random.randint(key, (), max(1, total - most), min(most, total - 1) + 1)
        return jnp.stack([one, total - one])
    tallies = jnp.asarray(split_up(count, total, most, skew), jnp.int32)
    pairs = (count - 1) // 2
    source_of, receiver = tallies[1:1 + 2 * pairs:2], tallies[2:2 + 2 * pairs:2]
    room = jnp.minimum(source_of - 1, most - receiver)
    shifted = jax.random.randint(jax.random.fold_in(key, 1), (pairs,), 0, 1 << 20) % (room + 1)
    tallies = tallies.at[1:1 + 2 * pairs:2].set(source_of - shifted).at[2:2 + 2 * pairs:2].set(receiver + shifted)
    return tallies[jax.random.permutation(jax.random.fold_in(key, 2), count)]


def gaussian(stream_key, shape, scale, most, cuts=(), kind=jnp.bfloat16):
    array = jax.random.normal(stream_key, shape, jnp.float32) * scale
    if len(cuts) > 0:
        array = block_scale(stream_key, shape, cuts, -0.22, 0.18) * array
    return jnp.clip(array, min=-most, max=most).astype(kind)


def setup_inputs(seed: int = 0) -> dict:
    streams_of = jax.random.split(jax.random.key(seed), 5)
    queries = draw_queries(jax.random.fold_in(streams_of[4], 71), 0)
    keys = draw_keys(jax.random.fold_in(streams_of[4], 71), 0)
    values = gaussian(streams_of[2], (TOKENS, KVH * HD), 1.0, 6.0, ((0, 512),))
    doc_lengths = uneven(streams_of[3], DOCS, TOKENS, MOST, 2).astype(jnp.int32)
    return dict(queries=queries, keys=keys, values=values, doc_lengths=doc_lengths)


def doc_index(positions, doc_ends):
    return lax.optimization_barrier(jnp.sum((doc_ends[None, :] <= positions[:, None]).astype(jnp.int32), axis=1))

def reference(queries, keys, values, doc_lengths):
    rows = TOK_DEV
    blocks = TOKENS // rows
    per_group = QH // KVH
    width = REACH * rows
    doc_ends = jnp.cumsum(doc_lengths).astype(jnp.int32)
    score_scale = 1.0 / math.sqrt(HD)
    q_all = queries.reshape(blocks, rows, KVH, per_group, HD)
    padded_keys = jnp.concatenate([jnp.zeros((width, KVH * HD), keys.dtype), keys], axis=0)
    padded_values = jnp.concatenate([jnp.zeros((width, KVH * HD), values.dtype), values], axis=0)

    def one_block(inputs):
        q_block, index = inputs
        start = (index * rows).astype(jnp.int32)
        k_window = lax.dynamic_slice_in_dim(padded_keys, start, width + rows, 0).reshape(width + rows, KVH, HD)
        v_window = lax.dynamic_slice_in_dim(padded_values, start, width + rows, 0).reshape(width + rows, KVH, HD)
        q_positions = start + jnp.arange(rows, dtype=jnp.int32)
        k_positions = start - width + jnp.arange(width + rows, dtype=jnp.int32)
        q_docs = doc_index(q_positions, doc_ends)
        k_docs = doc_index(k_positions, doc_ends)
        allowed = (q_docs[:, None] == k_docs[None, :]) & (k_positions[None, :] <= q_positions[:, None]) & (k_positions[None, :] >= 0)
        scores = jnp.einsum('qgjd,kgd->gjqk', q_block.astype(jnp.float32), k_window.astype(jnp.float32)) * score_scale
        masked = jnp.where(allowed[None, None], scores, -1e+30)
        maxima = lax.optimization_barrier(jnp.max(masked, axis=3, keepdims=True))
        weights = jnp.where(allowed[None, None], jnp.exp(scores - maxima), 0.0)
        totals = lax.optimization_barrier(jnp.sum(weights, axis=3))
        rounded = lax.optimization_barrier(weights.astype(jnp.bfloat16)).astype(jnp.float32)
        weighted = jnp.einsum('gjqk,kgd->qgjd', rounded, v_window.astype(jnp.float32))
        result = weighted / jnp.transpose(totals, (2, 0, 1))[..., None]
        return result.astype(jnp.bfloat16).reshape(rows, QH * HD)
    indices = jnp.arange(blocks, dtype=jnp.int32)
    return lax.map(one_block, (q_all, indices)).reshape(TOKENS, QH * HD)
```

```python
import functools
import math

import jax
import jax.numpy as jnp
from jax import lax
from jax.experimental import pallas as pl
from jax.experimental.pallas import tpu as pltpu
from jax.sharding import PartitionSpec as P

HD = 128
GROUPS = 2
PER = 4
HEADS = GROUPS * PER
CORES = 2
MASKED = -1e30
TILE = 128
SCALE = math.log2(math.e) / math.sqrt(HD)
VMEM = 40 * 1024 * 1024


def shifted(value, steps):
    count = lax.axis_size("ctx")
    return lax.ppermute(value, "ctx", [(at, at + steps) for at in range(count - steps)])


def both_cores(value):
    count = lax.axis_size("ctx")
    pairs = [[at + core for core in range(CORES)] for at in range(0, count, CORES)]
    return lax.all_gather(value, "ctx", axis=0, tiled=True, axis_index_groups=pairs)


def pack_kernel(k_ref, v_ref, out_ref):
    for kind, ref in enumerate((k_ref, v_ref)):
        for column in range(out_ref.shape[0] * GROUPS):
            part = ref[:, column * HD : (column + 1) * HD]
            out_ref[column // GROUPS, kind, column % GROUPS] = part


def pack(keys, values, targets):
    rows = keys.shape[0]
    return pl.pallas_call(
        pack_kernel,
        out_shape=jax.ShapeDtypeStruct((targets, 2, GROUPS, rows, HD), keys.dtype),
        name="pack",
    )(keys, values)


def query_tile(q_ref, group, row):
    heads = [
        q_ref[pl.ds(row, TILE), (group * PER + j) * HD : (group * PER + j + 1) * HD]
        for j in range(PER)
    ]
    return jnp.concatenate(heads, axis=0)


def chunk(kv_ref, kind, group, first, count):
    blocks = kv_ref[first : first + count, kind, group]
    return blocks.reshape(count * blocks.shape[1], HD)


def with_ones(values):
    return jnp.concatenate([values, jnp.ones_like(values)], axis=1)


def score(queries, keys, bias):
    raw = lax.dot_general(
        queries, keys, (((1,), (1,)), ((), ())), preferred_element_type=jnp.float32
    )
    return raw.reshape(PER, TILE, -1) + bias[None]


def weigh(raw, top, values):
    weights = jnp.exp2((raw - top) * SCALE).astype(jnp.bfloat16)
    summed = jnp.dot(
        weights.reshape(PER * TILE, -1), with_ones(values), preferred_element_type=jnp.float32
    )
    return summed.reshape(PER, TILE, 2 * HD)


def doc_starts(lengths_ref, starts_ref, first):
    lengths = lengths_ref[...]
    docs = lengths.shape[1]
    earlier = lax.broadcasted_iota(jnp.int32, (docs, docs), 0) < lax.broadcasted_iota(
        jnp.int32, (docs, docs), 1
    )
    earlier = earlier.astype(jnp.bfloat16)

    def before(part):
        part = jnp.broadcast_to(part.astype(jnp.float32), (16, docs)).astype(jnp.bfloat16)
        return jnp.dot(part, earlier, preferred_element_type=jnp.float32)[0:1]

    begins = before(lengths >> 4) * 16.0 + before(lengths & 15)
    rows = starts_ref.shape[0]
    for row in range(0, rows, TILE):
        at = lax.broadcasted_iota(jnp.int32, (TILE, docs), 0) + (first + row)
        at = at.astype(jnp.float32)
        found = jnp.max(jnp.where(begins <= at, begins, 0.0), axis=1, keepdims=True)
        starts_ref[row : row + TILE] = jnp.broadcast_to(found, (TILE, HD))


def own_kernel(lengths_ref, q_ref, kv_ref, starts_ref, acc_ref, sum_ref, top_ref):
    rows = q_ref.shape[0]
    part = kv_ref.shape[3]
    blocks = rows // part
    device = lax.axis_index("ctx")
    core = lax.rem(device, CORES)
    doc_starts(lengths_ref, starts_ref, device * rows)

    def run(earlier):
        for tile in range(rows // TILE):
            row = tile * TILE
            used = -(-(row + TILE) // part) + earlier * blocks
            keys = used * part
            at_key = lax.broadcasted_iota(jnp.int32, (TILE, keys), 1) - earlier * rows
            at_query = lax.broadcasted_iota(jnp.int32, (TILE, keys), 0) + row
            since = starts_ref[row : row + TILE, 0:1] - (device * rows).astype(jnp.float32)
            allowed = (at_key <= at_query) & (at_key.astype(jnp.float32) >= since)
            bias = jnp.where(allowed, 0.0, MASKED)
            for group in range(GROUPS):
                queries = query_tile(q_ref, group, row)
                raw = score(queries, chunk(kv_ref, 0, group, 0, used), bias)
                top = jnp.max(raw, axis=2, keepdims=True)
                summed = weigh(raw, top, chunk(kv_ref, 1, group, 0, used))
                heads = pl.ds(group * PER, PER)
                acc_ref[heads, row : row + TILE] = summed[:, :, :HD]
                sum_ref[heads, row : row + TILE] = summed[:, :, HD:]
                top_ref[heads, row : row + TILE] = jnp.broadcast_to(top, (PER, TILE, HD))

    for which in range(CORES):
        pl.when(core == which)(functools.partial(run, which))


def update(q_ref, kv_ref, starts_ref, state, tile, base, first, count):
    acc_ref, sum_ref, top_ref = state
    part = kv_ref.shape[3]
    row = tile * TILE
    at_key = lax.broadcasted_iota(jnp.int32, (TILE, count * part), 1) + (base + first * part)
    bias = jnp.where(at_key.astype(jnp.float32) >= starts_ref[row : row + TILE, 0:1], 0.0, MASKED)
    for group in range(GROUPS):
        heads = pl.ds(group * PER, PER)
        raw = score(query_tile(q_ref, group, row), chunk(kv_ref, 0, group, first, count), bias)
        old = top_ref[heads, row : row + TILE]
        top = jnp.maximum(old, jnp.max(raw, axis=2, keepdims=True))
        summed = weigh(raw, top[:, :, 0:1], chunk(kv_ref, 1, group, first, count))
        keep = jnp.exp2((old - top) * SCALE)
        yield heads, row, top, (
            acc_ref[heads, row : row + TILE] * keep + summed[:, :, :HD],
            sum_ref[heads, row : row + TILE] * keep + summed[:, :, HD:],
        )


def near_kernel(q_ref, kv_ref, starts_ref, acc_in, sum_in, top_in, acc_ref, sum_ref, top_ref):
    rows = q_ref.shape[0]
    chip = lax.div(lax.axis_index("ctx"), CORES)
    base = (chip - 1) * CORES * rows
    for tile in range(rows // TILE):
        parts = update(
            q_ref, kv_ref, starts_ref, (acc_in, sum_in, top_in), tile, base, 0, kv_ref.shape[0]
        )
        for heads, row, top, (acc, total) in parts:
            acc_ref[heads, row : row + TILE] = acc
            sum_ref[heads, row : row + TILE] = total
            top_ref[heads, row : row + TILE] = top


def far_kernel(q_ref, kv_ref, starts_ref, acc_in, sum_in, top_in, out_ref):
    rows = q_ref.shape[0]
    blocks, part = kv_ref.shape[0], kv_ref.shape[3]
    chip = lax.div(lax.axis_index("ctx"), CORES)
    base = (chip - 2) * CORES * rows
    end = (base + CORES * rows).astype(jnp.float32)

    def write(heads, row, acc, total):
        result = (acc / total).astype(out_ref.dtype)
        for j in range(PER):
            column = (heads.start + j) * HD
            out_ref[row : row + TILE, column : column + HD] = result[j]

    for tile in range(rows // TILE):
        row = tile * TILE
        needed = end - jnp.min(starts_ref[row : row + 8])
        steps = [0, blocks // 2, blocks]
        for low, high in zip(steps[:-1], steps[1:]):

            @pl.when((needed > low * part) & (needed <= high * part))
            def _():
                parts = update(
                    q_ref, kv_ref, starts_ref, (acc_in, sum_in, top_in), tile, base,
                    blocks - high, high,
                )
                for heads, row, _, (acc, total) in parts:
                    write(heads, row, acc, total)

        @pl.when(needed <= 0)
        def _():
            for group in range(GROUPS):
                heads = pl.ds(group * PER, PER)
                write(heads, row, acc_in[heads, row : row + TILE], sum_in[heads, row : row + TILE])


def cost(rows, keys):
    pairs = rows * keys * HEADS
    return pl.CostEstimate(
        flops=pairs * HD * 6, bytes_accessed=8 * rows * HEADS * HD, transcendentals=pairs
    )


def local(queries, keys, values, doc_lengths):
    rows = queries.shape[0]
    targets = lax.axis_size("head")
    packed = pack(keys, values, targets)
    own = lax.all_to_all(packed, "head", split_axis=0, concat_axis=0, tiled=True)
    first = shifted(own, CORES)
    own_both = both_cores(own)
    state = [jax.ShapeDtypeStruct((HEADS, rows, HD), jnp.float32)] * 3
    params = pltpu.CompilerParams(vmem_limit_bytes=VMEM)
    starts, *carried = pl.pallas_call(
        own_kernel,
        out_shape=[jax.ShapeDtypeStruct((rows, HD), jnp.float32)] + state,
        compiler_params=params,
        cost_estimate=cost(rows, 2 * rows),
        name="own",
    )(doc_lengths.reshape(1, -1), queries, own_both)
    second = shifted(first, CORES)
    first_both = both_cores(first)
    carried = pl.pallas_call(
        near_kernel,
        out_shape=state,
        compiler_params=params,
        cost_estimate=cost(rows, 2 * rows),
        name="near",
    )(queries, first_both, starts, *carried)
    second_both = both_cores(second)
    return pl.pallas_call(
        far_kernel,
        out_shape=jax.ShapeDtypeStruct(queries.shape, queries.dtype),
        compiler_params=params,
        cost_estimate=cost(rows, rows),
        name="far",
    )(queries, second_both, starts, *carried)


def solution(mesh):
    placed = (P("ctx", "head"), P(("ctx", "head"), None), P(("ctx", "head"), None), P())
    return jax.shard_map(
        local, mesh=mesh, in_specs=placed, out_specs=P("ctx", "head"), check_vma=False
    )
```

```python
import functools
import math

import jax
import jax.numpy as jnp
from jax import lax
from jax.experimental import pallas as pl
from jax.experimental.pallas import tpu as pltpu
from jax.sharding import PartitionSpec as P

HD = 128
GROUPS = 2
PER = 4
HEADS = GROUPS * PER
CORES = 2
MASKED = -1e30
TILE = 128
STEP = 256
SCALE = math.log2(math.e) / math.sqrt(HD)
VMEM = 40 * 1024 * 1024


def shifted(value, steps):
    count = lax.axis_size("ctx")
    return lax.ppermute(value, "ctx", [(at, at + steps) for at in range(count - steps)])


def both_cores(value):
    count = lax.axis_size("ctx")
    pairs = [[at + core for core in range(CORES)] for at in range(0, count, CORES)]
    return lax.all_gather(value, "ctx", axis=0, tiled=True, axis_index_groups=pairs)


def pack_kernel(k_ref, v_ref, out_ref):
    for kind, ref in enumerate((k_ref, v_ref)):
        for column in range(out_ref.shape[0] * GROUPS):
            part = ref[:, column * HD : (column + 1) * HD]
            out_ref[column // GROUPS, kind, column % GROUPS] = part


def pack(keys, values, targets):
    rows = keys.shape[0]
    return pl.pallas_call(
        pack_kernel,
        out_shape=jax.ShapeDtypeStruct((targets, 2, GROUPS, rows, HD), keys.dtype),
        name="pack",
    )(keys, values)


def chunk(kv_ref, kind, group, first, count):
    blocks, part = kv_ref.shape[0], kv_ref.shape[3]
    return kv_ref[:, kind, group].reshape(blocks * part, HD)[first : first + count]


def with_ones(values):
    return jnp.concatenate([values, jnp.ones_like(values)], axis=1)


def stacked(q_ref, group, rows):
    heads = range(group * PER, (group + 1) * PER)
    return jnp.concatenate([q_ref[rows, head * HD : (head + 1) * HD] for head in heads], axis=0)


def score(queries, keys):
    raw = lax.dot_general(
        queries, keys, (((1,), (1,)), ((), ())), preferred_element_type=jnp.float32
    )
    return raw.reshape(PER, TILE, keys.shape[0])


def weigh(raw, top):
    return jnp.exp2((raw - top) * SCALE).astype(jnp.bfloat16)


def total(weights, values):
    flat = weights.reshape(PER * TILE, values.shape[0])
    summed = jnp.dot(flat, with_ones(values), preferred_element_type=jnp.float32)
    return summed.reshape(PER, TILE, 2 * HD)


def doc_starts(lengths_ref, starts_ref, first):
    lengths = lengths_ref[...]
    docs = lengths.shape[1]
    earlier = lax.broadcasted_iota(jnp.int32, (docs, docs), 0) < lax.broadcasted_iota(
        jnp.int32, (docs, docs), 1
    )
    earlier = earlier.astype(jnp.bfloat16)

    def before(part):
        part = jnp.broadcast_to(part.astype(jnp.float32), (16, docs)).astype(jnp.bfloat16)
        return jnp.dot(part, earlier, preferred_element_type=jnp.float32)[0:1]

    begins = before(lengths >> 4) * 16.0 + before(lengths & 15)
    rows = starts_ref.shape[0]
    for row in range(0, rows, TILE):
        at = lax.broadcasted_iota(jnp.int32, (TILE, docs), 0) + (first + row)
        at = at.astype(jnp.float32)
        found = jnp.max(jnp.where(begins <= at, begins, 0.0), axis=1, keepdims=True)
        starts_ref[row : row + TILE] = jnp.broadcast_to(found, (TILE, HD))


def own_kernel(q_ref, kv_ref, lengths_ref, starts_ref, acc_ref, sum_ref, top_ref):
    rows = q_ref.shape[0]
    device = lax.axis_index("ctx")
    core = lax.rem(device, CORES)
    doc_starts(lengths_ref, starts_ref, device * rows)

    def run(earlier):
        for tile in range(rows // TILE):
            row = tile * TILE
            keys = -(-(row + TILE + earlier * rows) // STEP) * STEP
            at_key = lax.broadcasted_iota(jnp.int32, (TILE, keys), 1) - earlier * rows
            at_query = lax.broadcasted_iota(jnp.int32, (TILE, keys), 0) + row
            since = starts_ref[row : row + TILE, 0:1] - (device * rows).astype(jnp.float32)
            allowed = (at_key <= at_query) & (at_key.astype(jnp.float32) >= since)
            bias = jnp.where(allowed, 0.0, MASKED)
            raws, sums = [], []
            for group in range(GROUPS):
                queries = stacked(q_ref, group, pl.ds(row, TILE))
                raws.append(score(queries, chunk(kv_ref, 0, group, 0, keys)) + bias[None])
            tops = [jnp.max(raw, axis=2, keepdims=True) for raw in raws]
            weights = [weigh(raw, top) for raw, top in zip(raws, tops)]
            for group, part in enumerate(weights):
                sums.append(total(part, chunk(kv_ref, 1, group, 0, keys)))
            for group in range(GROUPS):
                heads = pl.ds(group * PER, PER)
                acc_ref[heads, row : row + TILE] = sums[group][:, :, :HD]
                sum_ref[heads, row : row + TILE] = sums[group][:, :, HD:]
                top_ref[heads, row : row + TILE] = jnp.broadcast_to(tops[group], (PER, TILE, HD))

    for which in range(CORES):
        pl.when(core == which)(functools.partial(run, which))


def update(q_ref, kv_ref, starts_ref, state, row, base, first, count):
    acc_ref, sum_ref, top_ref = state
    rows = pl.ds(row, TILE)
    at_key = lax.broadcasted_iota(jnp.int32, (TILE, count), 1) + (base + first)
    bias = jnp.where(at_key.astype(jnp.float32) >= starts_ref[rows, 0:1], 0.0, MASKED)
    raws, tops, sums = [], [], []
    for group in range(GROUPS):
        keys = chunk(kv_ref, 0, group, first, count)
        raws.append(score(stacked(q_ref, group, rows), keys) + bias[None])
    for group, raw in enumerate(raws):
        old = top_ref[pl.ds(group * PER, PER), rows]
        tops.append(jnp.maximum(old, jnp.max(raw, axis=2, keepdims=True)))
    weights = [weigh(raw, top[:, :, 0:1]) for raw, top in zip(raws, tops)]
    for group, part in enumerate(weights):
        sums.append(total(part, chunk(kv_ref, 1, group, first, count)))
    for head in range(HEADS):
        group, j = divmod(head, PER)
        keep = jnp.exp2((top_ref[head, rows] - tops[group][j]) * SCALE)
        acc = acc_ref[head, rows] * keep + sums[group][j][:, :HD]
        yield head, tops[group][j], acc, sum_ref[head, rows] * keep + sums[group][j][:, HD:]


def near_kernel(q_ref, kv_ref, starts_ref, acc_in, sum_in, top_in, acc_ref, sum_ref, top_ref):
    rows = q_ref.shape[0]
    chip = lax.div(lax.axis_index("ctx"), CORES)
    base = (chip - 1) * CORES * rows
    state = (acc_in, sum_in, top_in)
    @pl.loop(0, rows // TILE)
    def _(tile):
        row = pl.multiple_of(tile * TILE, TILE)
        parts = update(q_ref, kv_ref, starts_ref, state, row, base, 0, CORES * rows)
        for head, top, acc, summed in parts:
            acc_ref[head, pl.ds(row, TILE)] = acc
            sum_ref[head, pl.ds(row, TILE)] = summed
            top_ref[head, pl.ds(row, TILE)] = top


def far_kernel(q_ref, kv_ref, starts_ref, acc_in, sum_in, top_in, out_ref):
    rows = q_ref.shape[0]
    tiles = rows // TILE
    chip = lax.div(lax.axis_index("ctx"), CORES)
    base = (chip - 2) * CORES * rows
    end = (base + CORES * rows).astype(jnp.float32)
    state = (acc_in, sum_in, top_in)
    since = [jnp.min(starts_ref[tile * TILE : tile * TILE + 8]) for tile in range(tiles)]
    reaching = [(start < end).astype(jnp.int32) for start in since]
    reaching = functools.reduce(lambda one, two: one + two, reaching)
    needed = end - since[0]

    def write(head, row, acc, total):
        rough = pl.reciprocal(total, approx=True)
        result = acc * (rough * (2.0 - total * rough))
        out_ref[pl.ds(row, TILE), head * HD : (head + 1) * HD] = result.astype(out_ref.dtype)

    def finish(tile):
        row = pl.multiple_of(tile * TILE, TILE)
        for head in range(HEADS):
            write(head, row, acc_in[head, pl.ds(row, TILE)], sum_in[head, pl.ds(row, TILE)])

    def reach(used, tile):
        row = pl.multiple_of(tile * TILE, TILE)
        parts = update(q_ref, kv_ref, starts_ref, state, row, base, CORES * rows - used, used)
        for head, _, acc, total in parts:
            write(head, row, acc, total)

    for low in range(0, CORES * rows, STEP):
        inside = (needed > low) & (needed <= low + STEP)

        @pl.when(inside)
        def _():
            pl.loop(0, reaching)(functools.partial(reach, low + STEP))

    pl.loop(reaching, tiles)(finish)


def cost(rows, keys):
    pairs = rows * keys * HEADS
    return pl.CostEstimate(
        flops=pairs * HD * 6, bytes_accessed=8 * rows * HEADS * HD, transcendentals=pairs
    )


def call(kernel, name, out_shape, keys, *operands):
    rows = operands[0].shape[0]
    return pl.pallas_call(
        kernel,
        out_shape=out_shape,
        compiler_params=pltpu.CompilerParams(vmem_limit_bytes=VMEM),
        cost_estimate=cost(rows, keys),
        name=name,
    )(*operands)


def own_part(queries, kv, doc_lengths):
    rows = queries.shape[0]
    state = [jax.ShapeDtypeStruct((HEADS, rows, HD), jnp.float32)] * 3
    starts = jax.ShapeDtypeStruct((rows, HD), jnp.float32)
    return call(
        own_kernel, "own", [starts] + state, 2 * rows, queries, kv, doc_lengths.reshape(1, -1)
    )


def near_part(queries, kv, starts, *state):
    shapes = [jax.ShapeDtypeStruct(part.shape, part.dtype) for part in state]
    return call(near_kernel, "near", shapes, kv.shape[0] * kv.shape[3], queries, kv, starts, *state)


def far_part(queries, kv, starts, *state):
    out = jax.ShapeDtypeStruct(queries.shape, queries.dtype)
    return call(far_kernel, "far", out, queries.shape[0], queries, kv, starts, *state)


def attention(queries, own_both, first_both, second_both, doc_lengths):
    starts, *state = own_part(queries, own_both, doc_lengths)
    state = near_part(queries, first_both, starts, *state)
    return far_part(queries, second_both, starts, *state)


def local(queries, keys, values, doc_lengths):
    targets = lax.axis_size("head")
    packed = pack(keys, values, targets)
    own = lax.all_to_all(packed, "head", split_axis=0, concat_axis=0, tiled=True)
    first = shifted(own, CORES)
    starts, *state = own_part(queries, both_cores(own), doc_lengths)
    first, starts = lax.optimization_barrier((first, starts))
    second = shifted(first, CORES)
    state = near_part(queries, both_cores(first), starts, *state)
    return far_part(queries, both_cores(second), starts, *state)


def solution(mesh):
    placed = (P("ctx", "head"), P(("ctx", "head"), None), P(("ctx", "head"), None), P())
    return jax.shard_map(
        local, mesh=mesh, in_specs=placed, out_specs=P("ctx", "head"), check_vma=False
    )
```

```python
import functools
import math

import jax
import jax.numpy as jnp
from jax import lax
from jax.experimental import pallas as pl
from jax.experimental.pallas import tpu as pltpu
from jax.sharding import PartitionSpec as P

HD = 128
GROUPS = 2
PER = 4
HEADS = GROUPS * PER
CORES = 2
MASKED = -1e30
TILE = 128
STEP = 256
SCALE = math.log2(math.e) / math.sqrt(HD)
VMEM = 40 * 1024 * 1024


def shifted(value, steps):
    count = lax.axis_size("ctx")
    return lax.ppermute(value, "ctx", [(at, at + steps) for at in range(count - steps)])


def both_cores(value):
    count = lax.axis_size("ctx")
    pairs = [[at + core for core in range(CORES)] for at in range(0, count, CORES)]
    return lax.all_gather(value, "ctx", axis=0, tiled=True, axis_index_groups=pairs)


def moved(value, steps, turn):
    chips, heads = lax.axis_size("ctx") // CORES, lax.axis_size("head")
    pairs = [
        ((chip * CORES + core) * heads + head,
         ((chip + steps) * CORES + core) * heads + (head + turn(core)) % heads)
        for chip in range(chips - steps)
        for core in range(CORES)
        for head in range(heads)
    ]
    return lax.ppermute(value, ("ctx", "head"), pairs)


def pack_kernel(first_of, k_ref, v_ref, out_ref):
    targets = out_ref.shape[0]
    first = lax.axis_index("head") if first_of == "self" else 0
    for kind, ref in enumerate((k_ref, v_ref)):
        for slot in range(targets):
            target = lax.rem(first + slot, targets)
            for group in range(GROUPS):
                column = (target * GROUPS + group) * HD
                if first_of == "self":
                    column = pl.multiple_of(column, HD)
                out_ref[slot, kind, group] = ref[:, pl.ds(column, HD)]


def pack(keys, values, targets, first_of):
    rows = keys.shape[0]
    return pl.pallas_call(
        functools.partial(pack_kernel, first_of),
        out_shape=jax.ShapeDtypeStruct((targets, 2, GROUPS, rows, HD), keys.dtype),
        name="pack_" + first_of,
    )(keys, values)


def chunk(kv_ref, kind, group, first, count):
    if kv_ref.ndim == 5:
        rows = kv_ref[:, kind, group].reshape(-1, HD)
    else:
        heads = kv_ref.shape[0]
        here = lax.axis_index("head")
        turns = [lax.rem(here - source + heads, heads) for source in range(heads)]
        rows = jnp.concatenate(
            [kv_ref[turn, core, kind, group] for core in range(CORES) for turn in turns]
        )
    return rows[first : first + count]


def with_ones(values):
    return jnp.concatenate([values, jnp.ones_like(values)], axis=1)


def stacked(q_ref, group, rows):
    heads = range(group * PER, (group + 1) * PER)
    return jnp.concatenate([q_ref[rows, head * HD : (head + 1) * HD] for head in heads], axis=0)


def score(queries, keys):
    raw = lax.dot_general(
        queries, keys, (((1,), (1,)), ((), ())), preferred_element_type=jnp.float32
    )
    return raw.reshape(PER, TILE, keys.shape[0])


def weigh(raw, top):
    return jnp.exp2((raw - top) * SCALE).astype(jnp.bfloat16)


def total(weights, values):
    flat = weights.reshape(PER * TILE, values.shape[0])
    summed = jnp.dot(flat, with_ones(values), preferred_element_type=jnp.float32)
    return summed.reshape(PER, TILE, 2 * HD)


def doc_starts(lengths_ref, starts_ref, first):
    lengths = lengths_ref[...]
    docs = lengths.shape[1]
    earlier = lax.broadcasted_iota(jnp.int32, (docs, docs), 0) < lax.broadcasted_iota(
        jnp.int32, (docs, docs), 1
    )
    earlier = earlier.astype(jnp.bfloat16)

    def before(part):
        part = jnp.broadcast_to(part.astype(jnp.float32), (16, docs)).astype(jnp.bfloat16)
        return jnp.dot(part, earlier, preferred_element_type=jnp.float32)[0:1]

    begins = before(lengths >> 4) * 16.0 + before(lengths & 15)
    rows = starts_ref.shape[0]
    for row in range(0, rows, TILE):
        at = lax.broadcasted_iota(jnp.int32, (TILE, docs), 0) + (first + row)
        at = at.astype(jnp.float32)
        found = jnp.max(jnp.where(begins <= at, begins, 0.0), axis=1, keepdims=True)
        starts_ref[row : row + TILE] = jnp.broadcast_to(found, (TILE, HD))


def own_kernel(q_ref, kv_ref, lengths_ref, starts_ref, acc_ref, sum_ref, top_ref):
    rows = q_ref.shape[0]
    device = lax.axis_index("ctx")
    core = lax.rem(device, CORES)
    doc_starts(lengths_ref, starts_ref, device * rows)

    def run(earlier):
        for tile in range(rows // TILE):
            row = tile * TILE
            keys = -(-(row + TILE + earlier * rows) // STEP) * STEP
            at_key = lax.broadcasted_iota(jnp.int32, (TILE, keys), 1) - earlier * rows
            at_query = lax.broadcasted_iota(jnp.int32, (TILE, keys), 0) + row
            since = starts_ref[row : row + TILE, 0:1] - (device * rows).astype(jnp.float32)
            allowed = (at_key <= at_query) & (at_key.astype(jnp.float32) >= since)
            bias = jnp.where(allowed, 0.0, MASKED)
            raws, sums = [], []
            for group in range(GROUPS):
                queries = stacked(q_ref, group, pl.ds(row, TILE))
                raws.append(score(queries, chunk(kv_ref, 0, group, 0, keys)) + bias[None])
            tops = [jnp.max(raw, axis=2, keepdims=True) for raw in raws]
            weights = [weigh(raw, top) for raw, top in zip(raws, tops)]
            for group, part in enumerate(weights):
                sums.append(total(part, chunk(kv_ref, 1, group, 0, keys)))
            for group in range(GROUPS):
                heads = pl.ds(group * PER, PER)
                acc_ref[heads, row : row + TILE] = sums[group][:, :, :HD]
                sum_ref[heads, row : row + TILE] = sums[group][:, :, HD:]
                top_ref[heads, row : row + TILE] = jnp.broadcast_to(tops[group], (PER, TILE, HD))

    for which in range(CORES):
        pl.when(core == which)(functools.partial(run, which))


def update(q_ref, kv_ref, starts_ref, state, row, base, first, count):
    acc_ref, sum_ref, top_ref = state
    rows = pl.ds(row, TILE)
    at_key = lax.broadcasted_iota(jnp.int32, (TILE, count), 1) + (base + first)
    bias = jnp.where(at_key.astype(jnp.float32) >= starts_ref[rows, 0:1], 0.0, MASKED)
    raws, tops, sums = [], [], []
    for group in range(GROUPS):
        keys = chunk(kv_ref, 0, group, first, count)
        raws.append(score(stacked(q_ref, group, rows), keys) + bias[None])
    for group, raw in enumerate(raws):
        old = top_ref[pl.ds(group * PER, PER), rows]
        tops.append(jnp.maximum(old, jnp.max(raw, axis=2, keepdims=True)))
    weights = [weigh(raw, top[:, :, 0:1]) for raw, top in zip(raws, tops)]
    for group, part in enumerate(weights):
        sums.append(total(part, chunk(kv_ref, 1, group, first, count)))
    for head in range(HEADS):
        group, j = divmod(head, PER)
        keep = jnp.exp2((top_ref[head, rows] - tops[group][j]) * SCALE)
        acc = acc_ref[head, rows] * keep + sums[group][j][:, :HD]
        yield head, tops[group][j], acc, sum_ref[head, rows] * keep + sums[group][j][:, HD:]


def near_kernel(q_ref, kv_ref, starts_ref, acc_in, sum_in, top_in, acc_ref, sum_ref, top_ref):
    rows = q_ref.shape[0]
    chip = lax.div(lax.axis_index("ctx"), CORES)
    base = (chip - 1) * CORES * rows
    state = (acc_in, sum_in, top_in)
    @pl.loop(0, rows // TILE)
    def _(tile):
        row = pl.multiple_of(tile * TILE, TILE)
        parts = update(q_ref, kv_ref, starts_ref, state, row, base, 0, CORES * rows)
        for head, top, acc, summed in parts:
            acc_ref[head, pl.ds(row, TILE)] = acc
            sum_ref[head, pl.ds(row, TILE)] = summed
            top_ref[head, pl.ds(row, TILE)] = top


def far_kernel(q_ref, kv_ref, starts_ref, acc_in, sum_in, top_in, out_ref):
    rows = q_ref.shape[0]
    tiles = rows // TILE
    chip = lax.div(lax.axis_index("ctx"), CORES)
    base = (chip - 2) * CORES * rows
    end = (base + CORES * rows).astype(jnp.float32)
    state = (acc_in, sum_in, top_in)
    since = [jnp.min(starts_ref[tile * TILE : tile * TILE + 8]) for tile in range(tiles)]
    reaching = [(start < end).astype(jnp.int32) for start in since]
    reaching = functools.reduce(lambda one, two: one + two, reaching)
    needed = end - since[0]

    def write(head, row, acc, total):
        rough = pl.reciprocal(total, approx=True)
        result = acc * (rough * (2.0 - total * rough))
        out_ref[pl.ds(row, TILE), head * HD : (head + 1) * HD] = result.astype(out_ref.dtype)

    def finish(tile):
        row = pl.multiple_of(tile * TILE, TILE)
        for head in range(HEADS):
            write(head, row, acc_in[head, pl.ds(row, TILE)], sum_in[head, pl.ds(row, TILE)])

    def reach(used, tile):
        row = pl.multiple_of(tile * TILE, TILE)
        parts = update(q_ref, kv_ref, starts_ref, state, row, base, CORES * rows - used, used)
        for head, _, acc, total in parts:
            write(head, row, acc, total)

    for low in range(0, CORES * rows, STEP):
        inside = (needed > low) & (needed <= low + STEP)

        @pl.when(inside)
        def _():
            pl.loop(0, reaching)(functools.partial(reach, low + STEP))

    pl.loop(reaching, tiles)(finish)


def cost(rows, keys):
    pairs = rows * keys * HEADS
    return pl.CostEstimate(
        flops=pairs * HD * 6, bytes_accessed=8 * rows * HEADS * HD, transcendentals=pairs
    )


def call(kernel, name, out_shape, keys, *operands):
    rows = operands[0].shape[0]
    return pl.pallas_call(
        kernel,
        out_shape=out_shape,
        compiler_params=pltpu.CompilerParams(vmem_limit_bytes=VMEM),
        cost_estimate=cost(rows, keys),
        name=name,
    )(*operands)


def own_part(queries, kv, doc_lengths):
    rows = queries.shape[0]
    state = [jax.ShapeDtypeStruct((HEADS, rows, HD), jnp.float32)] * 3
    starts = jax.ShapeDtypeStruct((rows, HD), jnp.float32)
    return call(
        own_kernel, "own", [starts] + state, 2 * rows, queries, kv, doc_lengths.reshape(1, -1)
    )


def near_part(queries, kv, starts, *state):
    shapes = [jax.ShapeDtypeStruct(part.shape, part.dtype) for part in state]
    keys = CORES * queries.shape[0]
    return call(near_kernel, "near", shapes, keys, queries, kv, starts, *state)


def far_part(queries, kv, starts, *state):
    out = jax.ShapeDtypeStruct(queries.shape, queries.dtype)
    return call(far_kernel, "far", out, queries.shape[0], queries, kv, starts, *state)


def local(queries, keys, values, doc_lengths):
    heads = lax.axis_size("head")
    share = heads // CORES
    core = lax.rem(lax.axis_index("ctx"), CORES)
    turned = both_cores(pack(keys, values, heads, "self")[None])
    pieces = [
        lax.dynamic_index_in_dim(turned, core * share + j, axis=1, keepdims=False)
        for j in range(share)
    ]
    first = [moved(piece, 1, lambda core, j=j: core * share + j) for j, piece in enumerate(pieces)]
    packed = pack(keys, values, heads, "zero")
    own = lax.all_to_all(packed, "head", split_axis=0, concat_axis=0, tiled=True)
    first = jnp.stack(first)
    second = shifted(first, CORES)
    starts, *state = own_part(queries, both_cores(own), doc_lengths)
    state = near_part(queries, both_cores(first), starts, *state)
    return far_part(queries, both_cores(second), starts, *state)


def solution(mesh):
    placed = (P("ctx", "head"), P(("ctx", "head"), None), P(("ctx", "head"), None), P())
    return jax.shard_map(
        local, mesh=mesh, in_specs=placed, out_specs=P("ctx", "head"), check_vma=False
    )
```

```python
import functools
import math

import jax
import jax.numpy as jnp
from jax import lax
from jax.experimental import pallas as pl
from jax.experimental.pallas import tpu as pltpu
from jax.sharding import PartitionSpec as P

HD = 128
GROUPS = 2
PER = 4
HEADS = GROUPS * PER
CORES = 2
MASKED = -1e30
TILE = 128
STEP = 256
SCALE = math.log2(math.e) / math.sqrt(HD)
VMEM = 40 * 1024 * 1024


def shifted(value, steps):
    count = lax.axis_size("ctx")
    return lax.ppermute(value, "ctx", [(at, at + steps) for at in range(count - steps)])


def both_cores(value):
    count = lax.axis_size("ctx")
    pairs = [[at + core for core in range(CORES)] for at in range(0, count, CORES)]
    return lax.all_gather(value, "ctx", axis=0, tiled=True, axis_index_groups=pairs)


def moved(value, steps, turn):
    chips, heads = lax.axis_size("ctx") // CORES, lax.axis_size("head")
    pairs = [
        ((chip * CORES + core) * heads + head,
         ((chip + steps) * CORES + core) * heads + (head + turn(core)) % heads)
        for chip in range(chips - steps)
        for core in range(CORES)
        for head in range(heads)
    ]
    return lax.ppermute(value, ("ctx", "head"), pairs)


def to_chip(value):
    chips, heads = lax.axis_size("ctx") // CORES, lax.axis_size("head")
    size = CORES * heads
    groups = [[chip * size + at for at in range(size)] for chip in range(chips)]
    return lax.all_to_all(
        value, ("ctx", "head"), split_axis=0, concat_axis=0, tiled=True, axis_index_groups=groups
    )


def pack_kernel(k_ref, v_ref, turned_ref, out_ref):
    targets = turned_ref.shape[0]
    here = lax.axis_index("head")
    for kind, ref in enumerate((k_ref, v_ref)):
        for slot in range(targets):
            turned = lax.rem(here + slot, targets)
            for group in range(GROUPS):
                column = pl.multiple_of((turned * GROUPS + group) * HD, HD)
                turned_ref[slot, kind, group] = ref[:, pl.ds(column, HD)]
                column = (slot * GROUPS + group) * HD
                for core in range(CORES):
                    out_ref[core * targets + slot, kind, group] = ref[:, column : column + HD]


def pack(keys, values, targets):
    shapes = [
        jax.ShapeDtypeStruct((count, 2, GROUPS, keys.shape[0], HD), keys.dtype)
        for count in (targets, CORES * targets)
    ]
    return pl.pallas_call(pack_kernel, out_shape=shapes, name="pack")(keys, values)


def chunk(kv_ref, kind, group, first, count):
    if kv_ref.ndim == 5:
        rows = kv_ref[:, kind, group].reshape(-1, HD)
    else:
        heads = kv_ref.shape[0]
        here = lax.axis_index("head")
        turns = [lax.rem(here - source + heads, heads) for source in range(heads)]
        rows = jnp.concatenate(
            [kv_ref[turn, core, kind, group] for core in range(CORES) for turn in turns]
        )
    return rows[first : first + count]


def with_ones(values):
    return jnp.concatenate([values, jnp.ones_like(values)], axis=1)


def stacked(q_ref, group, rows):
    heads = range(group * PER, (group + 1) * PER)
    return jnp.concatenate([q_ref[rows, head * HD : (head + 1) * HD] for head in heads], axis=0)


def score(queries, keys):
    raw = lax.dot_general(
        queries, keys, (((1,), (1,)), ((), ())), preferred_element_type=jnp.float32
    )
    return raw.reshape(PER, TILE, keys.shape[0])


def weigh(raw, top):
    return jnp.exp2((raw - top) * SCALE).astype(jnp.bfloat16)


def total(weights, values):
    flat = weights.reshape(PER * TILE, values.shape[0])
    summed = jnp.dot(flat, with_ones(values), preferred_element_type=jnp.float32)
    return summed.reshape(PER, TILE, 2 * HD)


def doc_starts(lengths_ref, starts_ref, first):
    lengths = lengths_ref[...]
    docs = lengths.shape[1]
    earlier = lax.broadcasted_iota(jnp.int32, (docs, docs), 0) < lax.broadcasted_iota(
        jnp.int32, (docs, docs), 1
    )
    earlier = earlier.astype(jnp.bfloat16)

    def before(part):
        part = jnp.broadcast_to(part.astype(jnp.float32), (16, docs)).astype(jnp.bfloat16)
        return jnp.dot(part, earlier, preferred_element_type=jnp.float32)[0:1]

    begins = before(lengths >> 4) * 16.0 + before(lengths & 15)
    rows = starts_ref.shape[0]
    for row in range(0, rows, TILE):
        at = lax.broadcasted_iota(jnp.int32, (TILE, docs), 0) + (first + row)
        at = at.astype(jnp.float32)
        found = jnp.max(jnp.where(begins <= at, begins, 0.0), axis=1, keepdims=True)
        starts_ref[row : row + TILE] = jnp.broadcast_to(found, (TILE, HD))


def own_kernel(q_ref, kv_ref, lengths_ref, starts_ref, acc_ref, sum_ref, top_ref):
    rows = q_ref.shape[0]
    device = lax.axis_index("ctx")
    core = lax.rem(device, CORES)
    doc_starts(lengths_ref, starts_ref, device * rows)

    def run(earlier):
        for tile in range(rows // TILE):
            row = tile * TILE
            keys = -(-(row + TILE + earlier * rows) // STEP) * STEP
            at_key = lax.broadcasted_iota(jnp.int32, (TILE, keys), 1) - earlier * rows
            at_query = lax.broadcasted_iota(jnp.int32, (TILE, keys), 0) + row
            since = starts_ref[row : row + TILE, 0:1] - (device * rows).astype(jnp.float32)
            allowed = (at_key <= at_query) & (at_key.astype(jnp.float32) >= since)
            bias = jnp.where(allowed, 0.0, MASKED)
            raws, sums = [], []
            for group in range(GROUPS):
                queries = stacked(q_ref, group, pl.ds(row, TILE))
                raws.append(score(queries, chunk(kv_ref, 0, group, 0, keys)) + bias[None])
            tops = [jnp.max(raw, axis=2, keepdims=True) for raw in raws]
            weights = [weigh(raw, top) for raw, top in zip(raws, tops)]
            for group, part in enumerate(weights):
                sums.append(total(part, chunk(kv_ref, 1, group, 0, keys)))
            for group in range(GROUPS):
                heads = pl.ds(group * PER, PER)
                acc_ref[heads, row : row + TILE] = sums[group][:, :, :HD]
                sum_ref[heads, row : row + TILE] = sums[group][:, :, HD:]
                top_ref[heads, row : row + TILE] = jnp.broadcast_to(tops[group], (PER, TILE, HD))

    for which in range(CORES):
        pl.when(core == which)(functools.partial(run, which))


def update(q_ref, kv_ref, starts_ref, state, row, base, first, count):
    acc_ref, sum_ref, top_ref = state
    rows = pl.ds(row, TILE)
    at_key = lax.broadcasted_iota(jnp.int32, (TILE, count), 1) + (base + first)
    bias = jnp.where(at_key.astype(jnp.float32) >= starts_ref[rows, 0:1], 0.0, MASKED)
    raws, tops, sums = [], [], []
    for group in range(GROUPS):
        keys = chunk(kv_ref, 0, group, first, count)
        raws.append(score(stacked(q_ref, group, rows), keys) + bias[None])
    for group, raw in enumerate(raws):
        old = top_ref[pl.ds(group * PER, PER), rows]
        tops.append(jnp.maximum(old, jnp.max(raw, axis=2, keepdims=True)))
    weights = [weigh(raw, top[:, :, 0:1]) for raw, top in zip(raws, tops)]
    for group, part in enumerate(weights):
        sums.append(total(part, chunk(kv_ref, 1, group, first, count)))
    for head in range(HEADS):
        group, j = divmod(head, PER)
        keep = jnp.exp2((top_ref[head, rows] - tops[group][j]) * SCALE)
        acc = acc_ref[head, rows] * keep + sums[group][j][:, :HD]
        yield head, tops[group][j], acc, sum_ref[head, rows] * keep + sums[group][j][:, HD:]


def near_kernel(q_ref, kv_ref, starts_ref, acc_in, sum_in, top_in, acc_ref, sum_ref, top_ref):
    rows = q_ref.shape[0]
    chip = lax.div(lax.axis_index("ctx"), CORES)
    base = (chip - 1) * CORES * rows
    state = (acc_in, sum_in, top_in)
    @pl.loop(0, rows // TILE)
    def _(tile):
        row = pl.multiple_of(tile * TILE, TILE)
        parts = update(q_ref, kv_ref, starts_ref, state, row, base, 0, CORES * rows)
        for head, top, acc, summed in parts:
            acc_ref[head, pl.ds(row, TILE)] = acc
            sum_ref[head, pl.ds(row, TILE)] = summed
            top_ref[head, pl.ds(row, TILE)] = top


def far_kernel(q_ref, kv_ref, starts_ref, acc_in, sum_in, top_in, out_ref):
    rows = q_ref.shape[0]
    tiles = rows // TILE
    chip = lax.div(lax.axis_index("ctx"), CORES)
    base = (chip - 2) * CORES * rows
    end = (base + CORES * rows).astype(jnp.float32)
    state = (acc_in, sum_in, top_in)
    since = [jnp.min(starts_ref[tile * TILE : tile * TILE + 8]) for tile in range(tiles)]
    reaching = [(start < end).astype(jnp.int32) for start in since]
    reaching = functools.reduce(lambda one, two: one + two, reaching)
    needed = end - since[0]

    def write(head, row, acc, total):
        rough = pl.reciprocal(total, approx=True)
        result = acc * (rough * (2.0 - total * rough))
        out_ref[pl.ds(row, TILE), head * HD : (head + 1) * HD] = result.astype(out_ref.dtype)

    def finish(tile):
        row = pl.multiple_of(tile * TILE, TILE)
        for head in range(HEADS):
            write(head, row, acc_in[head, pl.ds(row, TILE)], sum_in[head, pl.ds(row, TILE)])

    def reach(used, tile):
        row = pl.multiple_of(tile * TILE, TILE)
        parts = update(q_ref, kv_ref, starts_ref, state, row, base, CORES * rows - used, used)
        for head, _, acc, total in parts:
            write(head, row, acc, total)

    for low in range(0, CORES * rows, STEP):
        inside = (needed > low) & (needed <= low + STEP)

        @pl.when(inside)
        def _():
            pl.loop(0, reaching)(functools.partial(reach, low + STEP))

    pl.loop(reaching, tiles)(finish)


def cost(rows, keys):
    pairs = rows * keys * HEADS
    return pl.CostEstimate(
        flops=pairs, bytes_accessed=rows * HD, transcendentals=0
    )


def call(kernel, name, out_shape, keys, *operands):
    rows = operands[0].shape[0]
    return pl.pallas_call(
        kernel,
        out_shape=out_shape,
        compiler_params=pltpu.CompilerParams(vmem_limit_bytes=VMEM),
        cost_estimate=cost(rows, keys),
        name=name,
    )(*operands)


def own_part(queries, kv, doc_lengths):
    rows = queries.shape[0]
    state = [jax.ShapeDtypeStruct((HEADS, rows, HD), jnp.float32)] * 3
    starts = jax.ShapeDtypeStruct((rows, HD), jnp.float32)
    return call(
        own_kernel, "own", [starts] + state, 2 * rows, queries, kv, doc_lengths.reshape(1, -1)
    )


def near_part(queries, kv, starts, *state):
    shapes = [jax.ShapeDtypeStruct(part.shape, part.dtype) for part in state]
    keys = CORES * queries.shape[0]
    return call(near_kernel, "near", shapes, keys, queries, kv, starts, *state)


def far_part(queries, kv, starts, *state):
    out = jax.ShapeDtypeStruct(queries.shape, queries.dtype)
    return call(far_kernel, "far", out, queries.shape[0], queries, kv, starts, *state)


def local(queries, keys, values, doc_lengths):
    heads = lax.axis_size("head")
    share = heads // CORES
    core = lax.rem(lax.axis_index("ctx"), CORES)
    turned, packed = pack(keys, values, heads)
    turned = both_cores(turned[None])
    turned, packed = lax.optimization_barrier((turned, packed))
    pieces = [
        lax.dynamic_index_in_dim(turned, core * share + j, axis=1, keepdims=False)
        for j in range(share)
    ]
    first = [moved(piece, 1, lambda core, j=j: core * share + j) for j, piece in enumerate(pieces)]
    own = to_chip(packed)
    first = jnp.stack(first)
    second = shifted(first, CORES)
    starts, *state = own_part(queries, own, doc_lengths)
    state = near_part(queries, both_cores(first), starts, *state)
    second, *state = lax.optimization_barrier((second, *state))
    return far_part(queries, both_cores(second), starts, *state)


def solution(mesh):
    placed = (P("ctx", "head"), P(("ctx", "head"), None), P(("ctx", "head"), None), P())
    return jax.shard_map(
        local, mesh=mesh, in_specs=placed, out_specs=P("ctx", "head"), check_vma=False
    )
```
